256 devices in a mesh: hid: 8 (over x, core), ffn: 32 (over y, z).
Axes of the slice: x: 4, y: 4, z: 8, core: 2. Of those that a mesh axis runs over, the one named last changes fastest.
Arguments:
- states: bfloat16 [512, 16384], P('ffn', 'hid'), may hold values from -6 to 6
- draft_lengths: int32 [64], replicated, may hold values from 1 to 8
- gate_weight: bfloat16 [16384, 28672], P('hid', 'ffn'), may hold values from -0.046875 to 0.046875
- up_weight: bfloat16 [16384, 28672], P('hid', 'ffn'), may hold values from -0.046875 to 0.046875
- down_weight: bfloat16 [28672, 16384], P('ffn', 'hid'), may hold values from -0.03125 to 0.03125
Outputs:
- mixed: float32 [512, 16384], P('ffn', 'hid')
The draws below stay inside these ranges and needn't reach their ends.
All inputs are finite; a program needn't handle non-finite values.
Results may differ from the reference program's by a relative error of at most 0.0029.
Values may be sent and summed in bfloat16 or wider, within the bound.
A program may use at most 64 MiB of HBM per device.

```python
import jax
import jax.numpy as jnp

D = 16384
FF = 28672
DRAFT = 8
ROWS = 512
ROLLOUTS = 64


def plant(result, stream_key, least, largest):
    spot = [jax.random.randint(jax.random.fold_in(stream_key, axis), (), 0, length) for axis, length in enumerate(result.shape)]
    main_axis = result.shape.index(max(result.shape))
    next_to = spot[:main_axis] + [(spot[main_axis] + 1) % result.shape[main_axis]] + spot[main_axis + 1:]
    return result.at[tuple(spot)].set(least).at[tuple(next_to)].set(largest)


def levels(key, extent, cuts, low, largest):
    loudness, own = 1.0, jax.random.fold_in(key, 6)
    for axis_at, blocks in cuts:
        draws = jnp.exp(jax.random.uniform(jax.random.fold_in(own, axis_at), (blocks,), jnp.float32, low / len(cuts), largest / len(cuts)))
        loudness = loudness * jnp.repeat(draws, extent[axis_at] // blocks).reshape([-1 if axis == axis_at else 1 for axis in range(len(extent))])
    return loudness


def scatter_about(stream_key, shape, width, bound, split=(), held_as=jnp.bfloat16):
    result = jax.random.normal(stream_key, shape, jnp.float32) * width
    if len(split) > 0:
        result = levels(stream_key, shape, split, -0.22, 0.18) * result
    return jnp.clip(result, min=-bound, max=bound).astype(held_as)


def setup_inputs(seed: int = 0) -> dict:
    key_list = jax.random.split(jax.random.key(seed), 6)
    return {
        "states": scatter_about(key_list[0], (ROWS, D), 1.0, 6.0, ((0, 32), (1, 8))),
        "draft_lengths": plant(jax.random.randint(key_list[1], (ROLLOUTS,), 1, DRAFT + 1), jax.random.fold_in(key_list[1], 1), 1, DRAFT).astype(jnp.int32),
        "gate_weight": scatter_about(key_list[2], (D, FF), D ** -0.5, 0.046875, ((0, 8), (1, 32))),
        "up_weight": scatter_about(key_list[3], (D, FF), D ** -0.5, 0.046875, ((0, 8), (1, 32))),
        "down_weight": scatter_about(key_list[4], (FF, D), FF ** -0.5, 0.03125, ((0, 32), (1, 8))),
    }


def reference(states, draft_lengths, gate_weight, up_weight, down_weight):
    live = (jnp.arange(DRAFT, dtype=jnp.int32)[None, :] < draft_lengths[:, None]).reshape(-1)
    gate = jnp.dot(states, gate_weight, preferred_element_type=jnp.float32)
    up_part = jnp.dot(states, up_weight, preferred_element_type=jnp.float32)
    hidden = jnp.where(live[:, None], jax.nn.silu(gate) * up_part, jnp.float32(0.0)).astype(jnp.bfloat16)
    return jnp.dot(hidden, down_weight, preferred_element_type=jnp.float32)
```

```python
import jax
import jax.numpy as jnp
from jax import lax
from jax.experimental import pallas as pl
from jax.experimental.pallas import tpu as pltpu
from jax.sharding import PartitionSpec as P

DRAFT = 8
NX, NY, NZ = 4, 4, 8
ROWS = 16
FEAT = 2048
UNITS = 896
BOTH = 2 * UNITS
OUT = 2048
TILE = 256
DY = (0, 1, 3, 2)
DZ_NEAR = (1, 7, 2, 6, 3, 5, 4)
DZ_FAR = (4, 3, 5, 2, 6, 1, 7, 0)


def kernel(
    lengths, states, gate_w, up_w, down_w, out,
    w1, wd, s, part, rc, xs, xr, h, own_out, op, yr, zs, zr,
    w_sem, s_sem, az_s, ay_s, af_s, a_r, c_s, c_r, x_s, x_r, hx_s, hx_r, hc_s, hc_r, y_s, y_r, z_s, z_r,
):
    hid, ffn = lax.axis_index("hid"), lax.axis_index("ffn")
    x, c = hid // 2, hid % 2
    y, z = ffn // NZ, ffn % NZ

    def at_z(dz):
        return (hid, y * NZ + (z + dz) % NZ)

    def at_y(dy):
        return (hid, ((y + dy) % NY) * NZ + z)

    def at_x(dx):
        return (((x + dx) % NX) * 2 + c, ffn)

    mate = (x * 2 + (1 - c), ffn)

    pending = []

    def send(src, dst, send_sem, recv_sem, device):
        copy = pltpu.make_async_remote_copy(src, dst, send_sem, recv_sem, device_id=device)
        copy.start()
        pending.append(copy)

    def arrived(dst, recv_sem):
        pltpu.make_async_remote_copy(dst, dst, w_sem.at[0], recv_sem, device_id=mate).wait_recv()

    mine = pltpu.make_async_copy(states, s.at[y, pl.ds(z * ROWS, ROWS)], s_sem)
    mine.start()
    loads = [
        pltpu.make_async_copy(gate_w, w1.at[:, pl.ds(0, UNITS)], w_sem.at[0]),
        pltpu.make_async_copy(up_w, w1.at[:, pl.ds(UNITS, UNITS)], w_sem.at[1]),
        pltpu.make_async_copy(down_w, wd, w_sem.at[2]),
    ]
    for load in loads:
        load.start()

    barrier = pltpu.get_barrier_semaphore()
    partners = [at_z(d) for d in range(1, NZ)] + [at_y(d) for d in range(1, NY)]
    partners += [at_x(d) for d in range(1, NX)] + [mate]
    for device in partners:
        pl.semaphore_signal(barrier, 1, device_id=device)
    pl.semaphore_wait(barrier, len(partners))
    mine.wait()

    def piece(ya, za):
        return s.at[ya, pl.ds(pl.multiple_of(za * ROWS, ROWS), ROWS)]

    def to_planes(n, za):
        for k, dy in enumerate((1, 3)):
            send(piece(y, za), piece(y, za), ay_s.at[n, k], a_r.at[y, za], at_y(dy))

    def far_plane(n, za):
        sy = (y + 3 + 2 * (za % 2)) % NY
        arrived(piece(sy, za), a_r.at[sy, za])
        dest = (hid, ((y + 1 + 2 * (za % 2)) % NY) * NZ + z)
        send(piece(sy, za), piece(sy, za), af_s.at[n], a_r.at[sy, za], dest)

    to_planes(0, z)
    for n, dz in enumerate(DZ_NEAR):
        send(piece(y, z), piece(y, z), az_s.at[n], a_r.at[y, z], at_z(dz))
    before = z
    for n, dz in enumerate(DZ_NEAR):
        za = (z + dz) % NZ
        arrived(piece(y, za), a_r.at[y, za])
        to_planes(n + 1, za)
        far_plane(n, before)
        before = za

    def first(i):
        ya = (y + DY[i]) % NY

        def tile(n, carry):
            columns = pl.ds(pl.multiple_of(n * TILE, TILE), TILE)
            r = jnp.dot(s[ya], w1[:, columns], preferred_element_type=jnp.float32)
            part[i, :, :, :, columns] = r.reshape(NX, 2, ROWS, TILE)
            return carry

        lax.fori_loop(0, BOTH // TILE, tile, 0)
        send(part.at[i, :, 1 - c], rc.at[i], c_s.at[i], c_r.at[i], mate)

    def over_x(i):
        arrived(rc.at[i], c_r.at[i])
        for dx in range(1, NX):
            xa = (x + dx) % NX
            xs[i, dx - 1] = part[i, xa, c] + rc[i, xa]
            send(xs.at[i, dx - 1], xr.at[i, dx - 1], x_s.at[i, dx - 1], x_r.at[i, dx - 1], at_x(dx))

    def activate(i):
        ya = (y + DY[i]) % NY
        for k in range(NX - 1):
            arrived(xr.at[i, k], x_r.at[i, k])
        both = part[i, x, c] + rc[i, x] + xr[i, 0] + xr[i, 1] + xr[i, 2]
        gate, up = both[:, :UNITS], both[:, UNITS:]
        owner = ya * NZ + hid
        row = lax.broadcasted_iota(jnp.int32, (ROWS, UNITS), 0)
        length = jnp.where(row < DRAFT, lengths[2 * owner], lengths[2 * owner + 1])
        value = gate / (1.0 + jnp.exp(-gate)) * up
        h[i, x, c] = jnp.where(row % DRAFT < length, value, 0.0).astype(jnp.bfloat16)
        for dx in range(1, NX):
            send(h.at[i, x, c], h.at[i, x, c], hx_s.at[i, dx - 1], hx_r.at[i, dx - 1], at_x(dx))

    def to_mate(i):
        for dx in range(1, NX):
            xa = (x + NX - dx) % NX
            arrived(h.at[i, xa, c], hx_r.at[i, dx - 1])
        send(h.at[i, :, c], h.at[i, :, c], hc_s.at[i], hc_r.at[i], mate)

    def second(i):
        arrived(h.at[i, :, 1 - c], hc_r.at[i])

        def tile(n, carry):
            columns = pl.ds(pl.multiple_of(n * TILE, TILE), TILE)
            rows = h[i].reshape(NX * 2 * ROWS, UNITS)
            r = jnp.dot(rows, wd[:, columns], preferred_element_type=jnp.float32)
            if i == 0:
                own_out[:, :, columns] = r.reshape(NZ, ROWS, TILE)
            else:
                op[i - 1, :, :, columns] = r.reshape(NZ, ROWS, TILE).astype(jnp.bfloat16)
            return carry

        lax.fori_loop(0, OUT // TILE, tile, 0)
        if i == 3:
            for n, dz in enumerate(DZ_FAR):
                za = (z + dz) % NZ
                send(op.at[2, za], yr.at[2, za], y_s.at[2, n], y_r.at[2, za], at_y(DY[i]))
        elif i > 0:
            send(op.at[i - 1], yr.at[i - 1], y_s.at[i - 1, 0], y_r.at[i - 1, 0], at_y(DY[i]))

    loads[0].wait()
    loads[1].wait()
    first(0)
    far_plane(7, before)
    for za in range(NZ):
        sy = (y + 1 + 2 * (za % 2)) % NY
        arrived(piece(sy, za), a_r.at[sy, za])
    first(1)
    over_x(0)
    first(2)
    over_x(1)
    for za in range(NZ):
        sy = (y + 2) % NY
        arrived(piece(sy, za), a_r.at[sy, za])
    first(3)
    over_x(2)
    activate(0)
    over_x(3)
    activate(1)
    to_mate(0)
    activate(2)
    to_mate(1)
    loads[2].wait()
    second(0)
    activate(3)
    to_mate(2)
    second(1)
    to_mate(3)
    second(2)
    second(3)

    arrived(yr.at[0], y_r.at[0, 0])
    arrived(yr.at[1], y_r.at[1, 0])
    for dz in DZ_FAR:
        za = (z + dz) % NZ
        arrived(yr.at[2, za], y_r.at[2, za])
        total = own_out[za]
        for k in range(3):
            total = total + yr[k, za].astype(jnp.float32)
        if dz:
            zs[dz - 1] = total.astype(jnp.bfloat16)
            send(zs.at[dz - 1], zr.at[dz - 1], z_s.at[dz - 1], z_r.at[dz - 1], at_z(dz))
        else:
            out[...] = total
    for k in range(NZ - 1):
        arrived(zr.at[k], z_r.at[k])
    total = out[...]
    for k in range(NZ - 1):
        total = total + zr[k].astype(jnp.float32)
    out[...] = total
    for copy in pending:
        copy.wait_send()


def local(states, draft_lengths, gate_weight, up_weight, down_weight):
    f32, bf16 = jnp.float32, jnp.bfloat16
    dma = pltpu.SemaphoreType.DMA
    hbm = pl.BlockSpec(memory_space=pl.ANY)
    return pl.pallas_call(
        kernel,
        out_shape=jax.ShapeDtypeStruct((ROWS, OUT), f32),
        in_specs=[pl.BlockSpec(memory_space=pltpu.SMEM), hbm, hbm, hbm, hbm],
        out_specs=pl.BlockSpec(memory_space=pltpu.VMEM),
        scratch_shapes=[
            pltpu.VMEM((FEAT, BOTH), bf16),
            pltpu.VMEM((UNITS, OUT), bf16),
            pltpu.VMEM((NY, NZ * ROWS, FEAT), bf16),
            pltpu.VMEM((4, NX, 2, ROWS, BOTH), f32),
            pltpu.VMEM((4, NX, ROWS, BOTH), f32),
            pltpu.VMEM((4, NX - 1, ROWS, BOTH), f32),
            pltpu.VMEM((4, NX - 1, ROWS, BOTH), f32),
            pltpu.VMEM((4, NX, 2, ROWS, UNITS), bf16),
            pltpu.VMEM((NZ, ROWS, OUT), f32),
            pltpu.VMEM((3, NZ, ROWS, OUT), bf16),
            pltpu.VMEM((3, NZ, ROWS, OUT), bf16),
            pltpu.VMEM((NZ - 1, ROWS, OUT), bf16),
            pltpu.VMEM((NZ - 1, ROWS, OUT), bf16),
            dma((3,)), dma, dma((7,)), dma((8, 2)), dma((8,)), dma((NY, NZ)),
            dma((4,)), dma((4,)), dma((4, 3)), dma((4, 3)), dma((4, 3)), dma((4, 3)),
            dma((4,)), dma((4,)), dma((3, 8)), dma((3, 8)), dma((7,)), dma((7,)),
        ],
        compiler_params=pltpu.CompilerParams(
            collective_id=0, has_side_effects=True, vmem_limit_bytes=56 << 20
        ),
        cost_estimate=pl.CostEstimate(
            flops=6 * 512 * FEAT * UNITS, bytes_accessed=6 * FEAT * UNITS, transcendentals=64 * UNITS
        ),
    )(draft_lengths, states, gate_weight, up_weight, down_weight)


def solution(mesh):
    placed = (P("ffn", "hid"), P(), P("hid", "ffn"), P("hid", "ffn"), P("ffn", "hid"))
    return jax.shard_map(
        local, mesh=mesh, in_specs=placed, out_specs=P("ffn", "hid"), check_vma=False
    )
```

```python
import jax
import jax.numpy as jnp
from jax import lax
from jax.experimental import pallas as pl
from jax.experimental.pallas import tpu as pltpu
from jax.sharding import PartitionSpec as P

DRAFT = 8
NX, NY, NZ = 4, 4, 8
ROWS = 16
FEAT = 2048
UNITS = 896
BOTH = 2 * UNITS
OUT = 2048
TILE = 256
DZ = (7, 0, 5, 2, 3, 4, 1, 6)
OWN = DZ.index(0)
DIRECT = (0, 5, 6, 7)
WIDE = 512
PEERS = ((2, 0), (2, 1), (1, 0), (3, 0), (1, 1), (3, 1), (0, 1))
POWER, SCALE = 7, 128.0


def coded(value):
    a = value * SCALE
    b = a * a * a
    return (b * b * a).astype(jnp.bfloat16)


def decoded(code):
    code = code.astype(jnp.float32)
    size = jnp.exp(jnp.log(jnp.abs(code)) * (1.0 / POWER)) * (1.0 / SCALE)
    return jnp.where(code == 0.0, 0.0, jnp.where(code < 0.0, -size, size))


def kernel(
    lengths, states, gate_w, up_w, down_w, out,
    w1, wd, s, part, rc, xs, xr, h, full, op, ym, mg, yr, zs, zr,
    w_sem, s_sem, az_s, ay_s, a_r, c_s, c_r, x_s, x_r, h_s, h_r, y_s, y_r, z_s, z_r,
):
    hid, ffn = lax.axis_index("hid"), lax.axis_index("ffn")
    x, c = hid // 2, hid % 2
    y, z = ffn // NZ, ffn % NZ

    def at_z(dz):
        return (hid, y * NZ + (z + dz) % NZ)

    def at_y(dy):
        return (hid, ((y + dy) % NY) * NZ + z)

    def at_x(dx):
        return (((x + dx) % NX) * 2 + c, ffn)

    mate = (x * 2 + (1 - c), ffn)
    peers = [(((x + dx) % NX) * 2 + (c + dc) % 2, ffn) for dx, dc in PEERS]

    pending = []

    def send(src, dst, send_sem, recv_sem, device):
        copy = pltpu.make_async_remote_copy(src, dst, send_sem, recv_sem, device_id=device)
        copy.start()
        pending.append(copy)

    def arrived(dst, recv_sem):
        pltpu.make_async_remote_copy(dst, dst, w_sem.at[0], recv_sem, device_id=mate).wait_recv()

    mine = pltpu.make_async_copy(states, s.at[OWN, y], s_sem)
    mine.start()
    loads = [
        pltpu.make_async_copy(gate_w, w1.at[:, pl.ds(0, UNITS)], w_sem.at[0]),
        pltpu.make_async_copy(up_w, w1.at[:, pl.ds(UNITS, UNITS)], w_sem.at[1]),
        pltpu.make_async_copy(down_w, wd, w_sem.at[2]),
    ]
    for load in loads:
        load.start()

    barrier = pltpu.get_barrier_semaphore()
    partners = [at_z(d) for d in range(1, NZ)] + [at_y(d) for d in range(1, NY)]
    partners += peers
    for device in partners:
        pl.semaphore_signal(barrier, 1, device_id=device)
    pl.semaphore_wait(barrier, len(partners))
    mine.wait()

    def to_planes(n):
        if n != OWN:
            arrived(s.at[n, y], a_r.at[n, 0])
        for dy in (2, 1, 3):
            send(s.at[n, y], s.at[n, y], ay_s.at[n, dy - 1], a_r.at[n, dy], at_y(dy))

    def first(n):
        for dy in (1, 3, 2):
            arrived(s.at[n, (y + NY - dy) % NY], a_r.at[n, dy])
        rows = s[n].reshape(NY * ROWS, FEAT)
        for at in range(0, BOTH, TILE):
            r = jnp.dot(rows, w1[:, at : at + TILE], preferred_element_type=jnp.float32)
            for k in range(2):
                low, high = max(at, k * UNITS), min(at + TILE, (k + 1) * UNITS)
                if low < high:
                    part[n, k, :, :, low - k * UNITS : high - k * UNITS] = r[:, low - at : high - at].reshape(
                        NY, ROWS, high - low
                    )
        send(part.at[n, :, :, :, window(1 - c)], rc.at[n], c_s.at[n], c_r.at[n], mate)

    def window(core):
        return pl.ds(pl.multiple_of(core * (UNITS - WIDE), 128), WIDE)

    def over_x(n):
        arrived(rc.at[n], c_r.at[n])
        for dx in (2, 1, 3):
            xa = (x + dx) % NX
            xs[n, dx - 1] = coded(part[n, :, xa, :, window(c)] + rc[n, :, xa])
            send(xs.at[n, dx - 1], xr.at[n, dx - 1], x_s.at[n, dx - 1], x_r.at[n, dx - 1], at_x(dx))

    def activate(n):
        for k in range(NX - 1):
            arrived(xr.at[n, k], x_r.at[n, k])
        both = part[n, :, x, :, window(c)] + rc[n, :, x]
        for k in range(NX - 1):
            both = both + decoded(xr[n, k])
        gate, up = both[0], both[1]
        owner = x * NZ + (z + DZ[n]) % NZ
        row = lax.broadcasted_iota(jnp.int32, (ROWS, WIDE), 0)
        length = jnp.where(row < DRAFT, lengths[2 * owner], lengths[2 * owner + 1])
        value = gate / (1.0 + jnp.exp(-gate)) * up
        h[n, c, x] = jnp.where(row % DRAFT < length, value, 0.0).astype(jnp.bfloat16)
        for k, device in enumerate(peers):
            send(h.at[n, c, x], h.at[n, c, x], h_s.at[n, k], h_r.at[n, k], device)

    def second(n):
        for k, (dx, dc) in enumerate(PEERS):
            arrived(h.at[n, (c + dc) % 2, (x + NX - dx) % NX], h_r.at[n, k])
        low = h[n, 0].reshape(NY * ROWS, WIDE)
        high = h[n, 1].reshape(NY * ROWS, WIDE)[:, 2 * WIDE - UNITS :]
        rows = jnp.concatenate([low, high], axis=1)
        for at in range(0, OUT, TILE):
            r = jnp.dot(rows, wd[:, at : at + TILE], preferred_element_type=jnp.float32)
            r = r.reshape(NY, ROWS, TILE)
            full[n, :, :, at : at + TILE] = r
            op[n, :, :, at : at + TILE] = r.astype(jnp.bfloat16)
        ahead, far, behind = (y + 1) % NY, (y + 2) % NY, (y + 3) % NY
        if n in DIRECT:
            for k, (dy, ya) in enumerate(((2, far), (1, ahead), (3, behind))):
                send(op.at[n, ya], yr.at[n, dy - 1], y_s.at[n, k], y_r.at[n, k], at_y(dy))
        else:
            left, right = pl.ds(0, OUT // 2), pl.ds(OUT // 2, OUT // 2)
            send(op.at[n, far, :, left], ym.at[n, 0], y_s.at[n, 0], y_r.at[n, 0], at_y(1))
            send(op.at[n, far, :, right], ym.at[n, 1], y_s.at[n, 1], y_r.at[n, 1], at_y(3))
            send(op.at[n, ahead, :, right], yr.at[n, 0, :, right], y_s.at[n, 2], y_r.at[n, 2], at_y(1))
            send(op.at[n, behind, :, left], yr.at[n, 1, :, left], y_s.at[n, 3], y_r.at[n, 3], at_y(3))

    def merge(n):
        for k in range(2):
            half = pl.ds(k * (OUT // 2), OUT // 2)
            arrived(ym.at[n, k], y_r.at[n, k])
            near = full[n, (y + 1 + 2 * k) % NY, :, half]
            mg[n, k] = (near + ym[n, k].astype(jnp.float32)).astype(jnp.bfloat16)
            send(mg.at[n, k], yr.at[n, k, :, half], y_s.at[n, 4 + k], y_r.at[n, 4 + k], at_y(1 + 2 * k))

    def over_y(n):
        total = full[n, y]
        if n in DIRECT:
            for k, dy in enumerate((2, 1, 3)):
                arrived(yr.at[n, dy - 1], y_r.at[n, k])
            total = total + yr[n, 2].astype(jnp.float32)
        else:
            for k in range(2):
                half, other = pl.ds(k * (OUT // 2), OUT // 2), pl.ds((1 - k) * (OUT // 2), OUT // 2)
                arrived(yr.at[n, k, :, other], y_r.at[n, 2 + k])
                arrived(yr.at[n, k, :, half], y_r.at[n, 4 + k])
        total = total + yr[n, 0].astype(jnp.float32) + yr[n, 1].astype(jnp.float32)
        if n != OWN:
            k = n - (n > OWN)
            zs[k] = total.astype(jnp.bfloat16)
            send(zs.at[k], zr.at[k], z_s.at[k], z_r.at[k], at_z(DZ[n]))
        else:
            out[...] = total

    for n in range(NZ):
        if n != OWN:
            send(s.at[OWN, y], s.at[n, y], az_s.at[n - (n > OWN)], a_r.at[n, 0], at_z(NZ - DZ[n]))
    to_planes(1)
    to_planes(0)
    loads[0].wait()
    loads[1].wait()
    first(1)
    to_planes(3)
    over_x(1)
    to_planes(2)
    first(0)
    to_planes(4)
    over_x(0)
    activate(1)
    first(3)
    to_planes(5)
    to_planes(7)
    first(2)
    over_x(3)
    activate(0)
    over_x(2)
    to_planes(6)
    loads[2].wait()
    second(1)
    first(4)
    activate(3)
    first(5)
    over_x(4)
    second(0)
    over_x(5)
    activate(2)
    first(7)
    second(3)
    activate(4)
    over_x(7)
    first(6)
    activate(5)
    merge(1)
    second(2)
    over_x(6)
    over_y(0)
    merge(3)
    second(4)
    activate(7)
    over_y(1)
    merge(2)
    second(5)
    over_y(3)
    activate(6)
    merge(4)
    over_y(2)
    second(7)
    over_y(5)
    second(6)
    over_y(4)
    over_y(7)
    over_y(6)
    for k in range(NZ - 1):
        arrived(zr.at[k], z_r.at[k])
    total = out[...]
    for k in range(NZ - 1):
        total = total + zr[k].astype(jnp.float32)
    out[...] = total
    for copy in pending:
        copy.wait_send()


def local(states, draft_lengths, gate_weight, up_weight, down_weight):
    f32, bf16 = jnp.float32, jnp.bfloat16
    dma = pltpu.SemaphoreType.DMA
    hbm = pl.BlockSpec(memory_space=pl.ANY)
    return pl.pallas_call(
        kernel,
        out_shape=jax.ShapeDtypeStruct((ROWS, OUT), f32),
        in_specs=[pl.BlockSpec(memory_space=pltpu.SMEM), hbm, hbm, hbm, hbm],
        out_specs=pl.BlockSpec(memory_space=pltpu.VMEM),
        scratch_shapes=[
            pltpu.VMEM((FEAT, BOTH), bf16),
            pltpu.VMEM((UNITS, OUT), bf16),
            pltpu.VMEM((NZ, NY, ROWS, FEAT), bf16),
            pltpu.VMEM((NZ, 2, NY, ROWS, UNITS), f32),
            pltpu.VMEM((NZ, 2, NY, ROWS, WIDE), f32),
            pltpu.VMEM((NZ, NX - 1, 2, ROWS, WIDE), bf16),
            pltpu.VMEM((NZ, NX - 1, 2, ROWS, WIDE), bf16),
            pltpu.VMEM((NZ, 2, NY, ROWS, WIDE), bf16),
            pltpu.VMEM((NZ, NY, ROWS, OUT), f32),
            pltpu.VMEM((NZ, NY, ROWS, OUT), bf16),
            pltpu.VMEM((NZ, 2, ROWS, OUT // 2), bf16),
            pltpu.VMEM((NZ, 2, ROWS, OUT // 2), bf16),
            pltpu.VMEM((NZ, 3, ROWS, OUT), bf16),
            pltpu.VMEM((NZ - 1, ROWS, OUT), bf16),
            pltpu.VMEM((NZ - 1, ROWS, OUT), bf16),
            dma((3,)), dma, dma((7,)), dma((8, 3)), dma((8, 4)),
            dma((8,)), dma((8,)), dma((8, 3)), dma((8, 3)), dma((8, 7)), dma((8, 7)),
            dma((8, 6)), dma((8, 6)), dma((7,)), dma((7,)),
        ],
        compiler_params=pltpu.CompilerParams(
            collective_id=0, has_side_effects=True, vmem_limit_bytes=56 << 20
        ),
        cost_estimate=pl.CostEstimate(
            flops=6 * 512 * FEAT * UNITS, bytes_accessed=6 * FEAT * UNITS, transcendentals=64 * UNITS
        ),
    )(draft_lengths, states, gate_weight, up_weight, down_weight)


def solution(mesh):
    placed = (P("ffn", "hid"), P(), P("hid", "ffn"), P("hid", "ffn"), P("ffn", "hid"))
    return jax.shard_map(
        local, mesh=mesh, in_specs=placed, out_specs=P("ffn", "hid"), check_vma=False
    )
```

```python
import jax
import jax.numpy as jnp
from jax import lax
from jax.experimental import pallas as pl
from jax.experimental.pallas import tpu as pltpu
from jax.sharding import PartitionSpec as P

DRAFT = 8
NX, NY, NZ = 4, 4, 8
ROWS = 16
FEAT = 2048
UNITS = 896
BOTH = 2 * UNITS
OUT = 2048
TILE = 256
DZ = (7, 0, 2, 5, 3, 4, 1, 6)
OWN = DZ.index(0)
DIRECT = (0, 5, 6, 7)
WIDE = 512
PEERS = ((2, 0), (2, 1), (1, 0), (3, 0), (1, 1), (3, 1), (0, 1))
POWER, SCALE = 7, 128.0


def coded(value):
    a = value * SCALE
    b = a * a * a
    return (b * b * a).astype(jnp.bfloat16)


def decoded(code):
    code = code.astype(jnp.float32)
    size = jnp.exp(jnp.log(jnp.abs(code)) * (1.0 / POWER)) * (1.0 / SCALE)
    return jnp.where(code == 0.0, 0.0, jnp.where(code < 0.0, -size, size))


def kernel(
    lengths, states, gate_w, up_w, down_w, out,
    w1, wd, s, part, rc, xs, xr, h, full, op, ym, mg, yr, zs, zr,
    w_sem, s_sem, az_s, ay_s, a_r, c_s, c_r, x_s, x_r, h_s, h_r, y_s, y_r, z_s, z_r,
):
    hid, ffn = lax.axis_index("hid"), lax.axis_index("ffn")
    x, c = hid // 2, hid % 2
    y, z = ffn // NZ, ffn % NZ

    def at_z(dz):
        return (hid, y * NZ + (z + dz) % NZ)

    def at_y(dy):
        return (hid, ((y + dy) % NY) * NZ + z)

    def at_x(dx):
        return (((x + dx) % NX) * 2 + c, ffn)

    mate = (x * 2 + (1 - c), ffn)
    peers = [(((x + dx) % NX) * 2 + (c + dc) % 2, ffn) for dx, dc in PEERS]

    pending = []

    def send(src, dst, send_sem, recv_sem, device):
        copy = pltpu.make_async_remote_copy(src, dst, send_sem, recv_sem, device_id=device)
        copy.start()
        pending.append(copy)

    def arrived(dst, recv_sem):
        pltpu.make_async_remote_copy(dst, dst, w_sem.at[0], recv_sem, device_id=mate).wait_recv()

    mine = pltpu.make_async_copy(states, s.at[OWN, y], s_sem)
    mine.start()
    loads = [
        pltpu.make_async_copy(gate_w, w1.at[:, pl.ds(0, UNITS)], w_sem.at[0]),
        pltpu.make_async_copy(up_w, w1.at[:, pl.ds(UNITS, UNITS)], w_sem.at[1]),
        pltpu.make_async_copy(down_w, wd, w_sem.at[2]),
    ]
    for load in loads:
        load.start()

    barrier = pltpu.get_barrier_semaphore()
    partners = [at_z(d) for d in range(1, NZ)] + [at_y(d) for d in range(1, NY)]
    partners += peers
    for device in partners:
        pl.semaphore_signal(barrier, 1, device_id=device)
    pl.semaphore_wait(barrier, len(partners))
    mine.wait()

    def to_planes(n):
        if n != OWN:
            arrived(s.at[n, y], a_r.at[n, 0])
        for dy in (2, 1, 3):
            send(s.at[n, y], s.at[n, y], ay_s.at[n, dy - 1], a_r.at[n, dy], at_y(dy))

    def first(*slots):
        for n in slots:
            for dy in (1, 3, 2):
                arrived(s.at[n, (y + NY - dy) % NY], a_r.at[n, dy])
        span = slice(slots[0], slots[-1] + 1)
        rows = s[span].reshape(len(slots) * NY * ROWS, FEAT)
        for at in range(0, BOTH, TILE):
            r = jnp.dot(rows, w1[:, at : at + TILE], preferred_element_type=jnp.float32)
            r = r.reshape(len(slots), NY, ROWS, TILE)
            for k in range(2):
                for core in range(2):
                    start = k * UNITS + core * (UNITS - WIDE)
                    low, high = max(at, start), min(at + TILE, start + WIDE)
                    if low < high:
                        part[span, core, k, :, :, low - start : high - start] = r[..., low - at : high - at]
        for n in slots:
            send(part.at[n, 1 - c], rc.at[n], c_s.at[n], c_r.at[n], mate)

    def over_x(n):
        arrived(rc.at[n], c_r.at[n])
        for dx in (2, 1, 3):
            xa = (x + dx) % NX
            xs[n, dx - 1] = coded(part[n, c, :, xa] + rc[n, :, xa])
            send(xs.at[n, dx - 1], xr.at[n, dx - 1], x_s.at[n, dx - 1], x_r.at[n, dx - 1], at_x(dx))

    def activate(n):
        for k in range(NX - 1):
            arrived(xr.at[n, k], x_r.at[n, k])
        both = part[n, c, :, x] + rc[n, :, x]
        for k in range(NX - 1):
            both = both + decoded(xr[n, k])
        gate, up = both[0], both[1]
        owner = x * NZ + (z + DZ[n]) % NZ
        row = lax.broadcasted_iota(jnp.int32, (ROWS, WIDE), 0)
        length = jnp.where(row < DRAFT, lengths[2 * owner], lengths[2 * owner + 1])
        value = gate / (1.0 + jnp.exp(-gate)) * up
        h[n, c, x] = jnp.where(row % DRAFT < length, value, 0.0).astype(jnp.bfloat16)
        for k, device in enumerate(peers):
            send(h.at[n, c, x], h.at[n, c, x], h_s.at[n, k], h_r.at[n, k], device)

    def second(n):
        for k, (dx, dc) in enumerate(PEERS):
            arrived(h.at[n, (c + dc) % 2, (x + NX - dx) % NX], h_r.at[n, k])
        low = h[n, 0].reshape(NY * ROWS, WIDE)
        high = h[n, 1].reshape(NY * ROWS, WIDE)[:, 2 * WIDE - UNITS :]
        rows = jnp.concatenate([low, high], axis=1)
        for at in range(0, OUT, TILE):
            r = jnp.dot(rows, wd[:, at : at + TILE], preferred_element_type=jnp.float32)
            r = r.reshape(NY, ROWS, TILE)
            full[n, :, :, at : at + TILE] = r
            op[n, :, :, at : at + TILE] = r.astype(jnp.bfloat16)
        ahead, far, behind = (y + 1) % NY, (y + 2) % NY, (y + 3) % NY
        if n in DIRECT:
            for k, (dy, ya) in enumerate(((2, far), (1, ahead), (3, behind))):
                send(op.at[n, ya], yr.at[n, dy - 1], y_s.at[n, k], y_r.at[n, k], at_y(dy))
        else:
            left, right = pl.ds(0, OUT // 2), pl.ds(OUT // 2, OUT // 2)
            send(op.at[n, far, :, left], ym.at[n, 0], y_s.at[n, 0], y_r.at[n, 0], at_y(1))
            send(op.at[n, far, :, right], ym.at[n, 1], y_s.at[n, 1], y_r.at[n, 1], at_y(3))
            send(op.at[n, ahead, :, right], yr.at[n, 0, :, right], y_s.at[n, 2], y_r.at[n, 2], at_y(1))
            send(op.at[n, behind, :, left], yr.at[n, 1, :, left], y_s.at[n, 3], y_r.at[n, 3], at_y(3))

    def merge(n):
        for k in range(2):
            half = pl.ds(k * (OUT // 2), OUT // 2)
            arrived(ym.at[n, k], y_r.at[n, k])
            near = full[n, (y + 1 + 2 * k) % NY, :, half]
            mg[n, k] = (near + ym[n, k].astype(jnp.float32)).astype(jnp.bfloat16)
            send(mg.at[n, k], yr.at[n, k, :, half], y_s.at[n, 4 + k], y_r.at[n, 4 + k], at_y(1 + 2 * k))

    def over_y(n):
        total = full[n, y]
        if n in DIRECT:
            for k, dy in enumerate((2, 1, 3)):
                arrived(yr.at[n, dy - 1], y_r.at[n, k])
            total = total + yr[n, 2].astype(jnp.float32)
        else:
            pass
            for k in range(2):
                half, other = pl.ds(k * (OUT // 2), OUT // 2), pl.ds((1 - k) * (OUT // 2), OUT // 2)
                arrived(yr.at[n, k, :, other], y_r.at[n, 2 + k])
                arrived(yr.at[n, k, :, half], y_r.at[n, 4 + k])
        total = total + yr[n, 0].astype(jnp.float32) + yr[n, 1].astype(jnp.float32)
        if n != OWN:
            k = n - (n > OWN)
            zs[k] = total.astype(jnp.bfloat16)
            send(zs.at[k], zr.at[k], z_s.at[k], z_r.at[k], at_z(DZ[n]))
        else:
            out[...] = total

    for n in range(NZ):
        if n != OWN:
            send(s.at[OWN, y], s.at[n, y], az_s.at[n - (n > OWN)], a_r.at[n, 0], at_z(NZ - DZ[n]))
    to_planes(1)
    to_planes(0)
    to_planes(2)
    loads[0].wait()
    loads[1].wait()
    first(1)
    over_x(1)
    to_planes(3)
    first(0)
    to_planes(4)
    over_x(0)
    first(2)
    activate(1)
    to_planes(5)
    to_planes(7)
    to_planes(6)
    over_x(2)
    first(3)
    activate(0)
    first(4)
    over_x(3)
    loads[2].wait()
    second(1)
    activate(2)
    over_x(4)
    first(5)
    second(0)
    over_x(5)
    activate(3)
    first(7)
    second(2)
    activate(4)
    merge(1)
    over_x(7)
    first(6)
    activate(5)
    second(3)
    over_x(6)
    over_y(0)
    merge(2)
    second(4)
    over_y(1)
    activate(7)
    merge(3)
    second(5)
    over_y(2)
    activate(6)
    merge(4)
    second(7)
    over_y(3)
    over_y(5)
    second(6)
    over_y(4)
    over_y(7)
    over_y(6)
    for copy in pending:
        copy.wait_send()
    total = out[...]
    for k in range(NZ - 1):
        arrived(zr.at[k], z_r.at[k])
        total = total + zr[k].astype(jnp.float32)
    out[...] = total


def local(states, draft_lengths, gate_weight, up_weight, down_weight):
    f32, bf16 = jnp.float32, jnp.bfloat16
    dma = pltpu.SemaphoreType.DMA
    hbm = pl.BlockSpec(memory_space=pl.ANY)
    return pl.pallas_call(
        kernel,
        out_shape=jax.ShapeDtypeStruct((ROWS, OUT), f32),
        in_specs=[pl.BlockSpec(memory_space=pltpu.SMEM), hbm, hbm, hbm, hbm],
        out_specs=pl.BlockSpec(memory_space=pltpu.VMEM),
        scratch_shapes=[
            pltpu.VMEM((FEAT, BOTH), bf16),
            pltpu.VMEM((UNITS, OUT), bf16),
            pltpu.VMEM((NZ, NY, ROWS, FEAT), bf16),
            pltpu.VMEM((NZ, 2, 2, NY, ROWS, WIDE), f32),
            pltpu.VMEM((NZ, 2, NY, ROWS, WIDE), f32),
            pltpu.VMEM((NZ, NX - 1, 2, ROWS, WIDE), bf16),
            pltpu.VMEM((NZ, NX - 1, 2, ROWS, WIDE), bf16),
            pltpu.VMEM((NZ, 2, NY, ROWS, WIDE), bf16),
            pltpu.VMEM((NZ, NY, ROWS, OUT), f32),
            pltpu.VMEM((NZ, NY, ROWS, OUT), bf16),
            pltpu.VMEM((NZ, 2, ROWS, OUT // 2), bf16),
            pltpu.VMEM((NZ, 2, ROWS, OUT // 2), bf16),
            pltpu.VMEM((NZ, 3, ROWS, OUT), bf16),
            pltpu.VMEM((NZ - 1, ROWS, OUT), bf16),
            pltpu.VMEM((NZ - 1, ROWS, OUT), bf16),
            dma((3,)), dma, dma((7,)), dma((8, 3)), dma((8, 4)),
            dma((8,)), dma((8,)), dma((8, 3)), dma((8, 3)), dma((8, 7)), dma((8, 7)),
            dma((8, 6)), dma((8, 6)), dma((7,)), dma((7,)),
        ],
        compiler_params=pltpu.CompilerParams(
            collective_id=0, has_side_effects=True, vmem_limit_bytes=56 << 20
        ),
        cost_estimate=pl.CostEstimate(
            flops=6 * 512 * FEAT * UNITS, bytes_accessed=6 * FEAT * UNITS, transcendentals=64 * UNITS
        ),
    )(draft_lengths, states, gate_weight, up_weight, down_weight)


def solution(mesh):
    placed = (P("ffn", "hid"), P(), P("hid", "ffn"), P("hid", "ffn"), P("ffn", "hid"))
    return jax.shard_map(
        local, mesh=mesh, in_specs=placed, out_specs=P("ffn", "hid"), check_vma=False
    )
```

```python
import jax
import jax.numpy as jnp
from jax import lax
from jax.experimental import pallas as pl
from jax.experimental.pallas import tpu as pltpu
from jax.sharding import PartitionSpec as P

DRAFT = 8
NX, NY, NZ = 4, 4, 8
ROWS = 16
FEAT = 2048
UNITS = 896
BOTH = 2 * UNITS
OUT = 2048
TILE = 256
DZ = (7, 0, 2, 5, 3, 4, 1, 6)
OWN = DZ.index(0)
DIRECT = (0, 5, 6, 7)
WIDE = 512
PEERS = ((2, 0), (2, 1), (1, 0), (3, 0), (1, 1), (3, 1), (0, 1))
POWER, SCALE = 7, 128.0


def coded(value):
    a = value * SCALE
    b = a * a * a
    return (b * b * a).astype(jnp.bfloat16)


def decoded(code):
    code = code.astype(jnp.float32)
    size = jnp.exp(jnp.log(jnp.abs(code)) * (1.0 / POWER)) * (1.0 / SCALE)
    return jnp.where(code == 0.0, 0.0, jnp.where(code < 0.0, -size, size))


def kernel(
    lengths, states, gate_w, up_w, down_w, out, others,
    w1, wd, s, part, rc, xs, xr, h, full, op, ym, mg, yr, zs, zr,
    w_sem, s_sem, az_s, ay_s, a_r, c_s, c_r, x_s, x_r, h_s, h_r, y_s, y_r, z_s, z_r,
):
    hid, ffn = lax.axis_index("hid"), lax.axis_index("ffn")
    x, c = hid // 2, hid % 2
    y, z = ffn // NZ, ffn % NZ

    def at_z(dz):
        return (hid, y * NZ + (z + dz) % NZ)

    def at_y(dy):
        return (hid, ((y + dy) % NY) * NZ + z)

    def at_x(dx):
        return (((x + dx) % NX) * 2 + c, ffn)

    mate = (x * 2 + (1 - c), ffn)
    peers = [(((x + dx) % NX) * 2 + (c + dc) % 2, ffn) for dx, dc in PEERS]

    pending = []

    def send(src, dst, send_sem, recv_sem, device):
        copy = pltpu.make_async_remote_copy(src, dst, send_sem, recv_sem, device_id=device)
        copy.start()
        pending.append(copy)

    def arrived(dst, recv_sem):
        pltpu.make_async_remote_copy(dst, dst, w_sem.at[0], recv_sem, device_id=mate).wait_recv()

    mine = pltpu.make_async_copy(states, s.at[OWN, y], s_sem)
    mine.start()
    loads = [
        pltpu.make_async_copy(gate_w, w1.at[:, pl.ds(0, UNITS)], w_sem.at[0]),
        pltpu.make_async_copy(up_w, w1.at[:, pl.ds(UNITS, UNITS)], w_sem.at[1]),
        pltpu.make_async_copy(down_w, wd, w_sem.at[2]),
    ]
    for load in loads:
        load.start()

    barrier = pltpu.get_barrier_semaphore()
    partners = [at_z(d) for d in range(1, NZ)] + [at_y(d) for d in range(1, NY)]
    partners += peers
    for device in partners:
        pl.semaphore_signal(barrier, 1, device_id=device)
    pl.semaphore_wait(barrier, len(partners))
    mine.wait()

    def to_planes(n):
        if n != OWN:
            arrived(s.at[n, y], a_r.at[n, 0])
        for dy in (2, 1, 3):
            send(s.at[n, y], s.at[n, y], ay_s.at[n, dy - 1], a_r.at[n, dy], at_y(dy))

    def first(*slots):
        for n in slots:
            for dy in (1, 3, 2):
                arrived(s.at[n, (y + NY - dy) % NY], a_r.at[n, dy])
        span = slice(slots[0], slots[-1] + 1)
        rows = s[span].reshape(len(slots) * NY * ROWS, FEAT)
        for at in range(0, BOTH, TILE):
            r = jnp.dot(rows, w1[:, at : at + TILE], preferred_element_type=jnp.float32)
            r = r.reshape(len(slots), NY, ROWS, TILE)
            for k in range(2):
                for core in range(2):
                    start = k * UNITS + core * (UNITS - WIDE)
                    low, high = max(at, start), min(at + TILE, start + WIDE)
                    if low < high:
                        part[span, core, k, :, :, low - start : high - start] = r[..., low - at : high - at]
        for n in slots:
            send(part.at[n, 1 - c], rc.at[n], c_s.at[n], c_r.at[n], mate)

    def over_x(n):
        arrived(rc.at[n], c_r.at[n])
        for dx in (2, 1, 3):
            xa = (x + dx) % NX
            xs[n, dx - 1] = coded(part[n, c, :, xa] + rc[n, :, xa])
            send(xs.at[n, dx - 1], xr.at[n, dx - 1], x_s.at[n, dx - 1], x_r.at[n, dx - 1], at_x(dx))

    def activate(n):
        for k in range(NX - 1):
            arrived(xr.at[n, k], x_r.at[n, k])
        both = part[n, c, :, x] + rc[n, :, x]
        for k in range(NX - 1):
            both = both + decoded(xr[n, k])
        gate, up = both[0], both[1]
        owner = x * NZ + (z + DZ[n]) % NZ
        row = lax.broadcasted_iota(jnp.int32, (ROWS, WIDE), 0)
        length = jnp.where(row < DRAFT, lengths[2 * owner], lengths[2 * owner + 1])
        value = gate / (1.0 + jnp.exp(-gate)) * up
        h[n, c, x] = jnp.where(row % DRAFT < length, value, 0.0).astype(jnp.bfloat16)
        for k, device in enumerate(peers):
            send(h.at[n, c, x], h.at[n, c, x], h_s.at[n, k], h_r.at[n, k], device)

    def second(n):
        for k, (dx, dc) in enumerate(PEERS):
            arrived(h.at[n, (c + dc) % 2, (x + NX - dx) % NX], h_r.at[n, k])
        low = h[n, 0].reshape(NY * ROWS, WIDE)
        high = h[n, 1].reshape(NY * ROWS, WIDE)[:, 2 * WIDE - UNITS :]
        rows = jnp.concatenate([low, high], axis=1)
        for at in range(0, OUT, TILE):
            r = jnp.dot(rows, wd[:, at : at + TILE], preferred_element_type=jnp.float32)
            r = r.reshape(NY, ROWS, TILE)
            full[n, :, :, at : at + TILE] = r
            op[n, :, :, at : at + TILE] = r.astype(jnp.bfloat16)
        ahead, far, behind = (y + 1) % NY, (y + 2) % NY, (y + 3) % NY
        if n in DIRECT:
            for k, (dy, ya) in enumerate(((2, far), (1, ahead), (3, behind))):
                send(op.at[n, ya], yr.at[n, dy - 1], y_s.at[n, k], y_r.at[n, k], at_y(dy))
        else:
            left, right = pl.ds(0, OUT // 2), pl.ds(OUT // 2, OUT // 2)
            send(op.at[n, far, :, left], ym.at[n, 0], y_s.at[n, 0], y_r.at[n, 0], at_y(1))
            send(op.at[n, far, :, right], ym.at[n, 1], y_s.at[n, 1], y_r.at[n, 1], at_y(3))
            send(op.at[n, ahead, :, right], yr.at[n, 0, :, right], y_s.at[n, 2], y_r.at[n, 2], at_y(1))
            send(op.at[n, behind, :, left], yr.at[n, 1, :, left], y_s.at[n, 3], y_r.at[n, 3], at_y(3))

    def merge(n):
        for k in range(2):
            half = pl.ds(k * (OUT // 2), OUT // 2)
            arrived(ym.at[n, k], y_r.at[n, k])
            near = full[n, (y + 1 + 2 * k) % NY, :, half]
            mg[n, k] = (near + ym[n, k].astype(jnp.float32)).astype(jnp.bfloat16)
            send(mg.at[n, k], yr.at[n, k, :, half], y_s.at[n, 4 + k], y_r.at[n, 4 + k], at_y(1 + 2 * k))

    def over_y(n):
        total = full[n, y]
        if n in DIRECT:
            for k, dy in enumerate((2, 1, 3)):
                arrived(yr.at[n, dy - 1], y_r.at[n, k])
            total = total + yr[n, 2].astype(jnp.float32)
        else:
            pass
            for k in range(2):
                half, other = pl.ds(k * (OUT // 2), OUT // 2), pl.ds((1 - k) * (OUT // 2), OUT // 2)
                arrived(yr.at[n, k, :, other], y_r.at[n, 2 + k])
                arrived(yr.at[n, k, :, half], y_r.at[n, 4 + k])
        total = total + yr[n, 0].astype(jnp.float32) + yr[n, 1].astype(jnp.float32)
        if n != OWN:
            k = n - (n > OWN)
            zs[k] = total.astype(jnp.bfloat16)
            send(zs.at[k], zr.at[k], z_s.at[k], z_r.at[k], at_z(DZ[n]))
        else:
            out[...] = total

    for n in range(NZ):
        if n != OWN:
            send(s.at[OWN, y], s.at[n, y], az_s.at[n - (n > OWN)], a_r.at[n, 0], at_z(NZ - DZ[n]))
    to_planes(1)
    to_planes(0)
    to_planes(2)
    loads[0].wait()
    loads[1].wait()
    first(1)
    over_x(1)
    to_planes(3)
    first(0)
    to_planes(4)
    over_x(0)
    first(2)
    activate(1)
    to_planes(5)
    to_planes(7)
    to_planes(6)
    over_x(2)
    first(3)
    activate(0)
    first(4)
    over_x(3)
    loads[2].wait()
    second(1)
    activate(2)
    over_x(4)
    first(5)
    second(0)
    over_x(5)
    activate(3)
    first(7)
    second(2)
    activate(4)
    merge(1)
    over_x(7)
    first(6)
    activate(5)
    second(3)
    over_x(6)
    over_y(0)
    merge(2)
    second(4)
    over_y(1)
    activate(7)
    merge(3)
    second(5)
    over_y(2)
    activate(6)
    merge(4)
    second(7)
    over_y(3)
    over_y(5)
    second(6)
    over_y(4)
    over_y(7)
    over_y(6)
    for copy in pending:
        copy.wait_send()
    total = jnp.zeros((ROWS, OUT), jnp.float32)
    for k in range(NZ - 1):
        arrived(zr.at[k], z_r.at[k])
        total = total + zr[k].astype(jnp.float32)
    others[...] = total


def local(states, draft_lengths, gate_weight, up_weight, down_weight):
    f32, bf16 = jnp.float32, jnp.bfloat16
    dma = pltpu.SemaphoreType.DMA
    hbm = pl.BlockSpec(memory_space=pl.ANY)
    own, others = pl.pallas_call(
        kernel,
        out_shape=[jax.ShapeDtypeStruct((ROWS, OUT), f32)] * 2,
        in_specs=[pl.BlockSpec(memory_space=pltpu.SMEM), hbm, hbm, hbm, hbm],
        out_specs=[pl.BlockSpec(memory_space=pltpu.VMEM)] * 2,
        scratch_shapes=[
            pltpu.VMEM((FEAT, BOTH), bf16),
            pltpu.VMEM((UNITS, OUT), bf16),
            pltpu.VMEM((NZ, NY, ROWS, FEAT), bf16),
            pltpu.VMEM((NZ, 2, 2, NY, ROWS, WIDE), f32),
            pltpu.VMEM((NZ, 2, NY, ROWS, WIDE), f32),
            pltpu.VMEM((NZ, NX - 1, 2, ROWS, WIDE), bf16),
            pltpu.VMEM((NZ, NX - 1, 2, ROWS, WIDE), bf16),
            pltpu.VMEM((NZ, 2, NY, ROWS, WIDE), bf16),
            pltpu.VMEM((NZ, NY, ROWS, OUT), f32),
            pltpu.VMEM((NZ, NY, ROWS, OUT), bf16),
            pltpu.VMEM((NZ, 2, ROWS, OUT // 2), bf16),
            pltpu.VMEM((NZ, 2, ROWS, OUT // 2), bf16),
            pltpu.VMEM((NZ, 3, ROWS, OUT), bf16),
            pltpu.VMEM((NZ - 1, ROWS, OUT), bf16),
            pltpu.VMEM((NZ - 1, ROWS, OUT), bf16),
            dma((3,)), dma, dma((7,)), dma((8, 3)), dma((8, 4)),
            dma((8,)), dma((8,)), dma((8, 3)), dma((8, 3)), dma((8, 7)), dma((8, 7)),
            dma((8, 6)), dma((8, 6)), dma((7,)), dma((7,)),
        ],
        compiler_params=pltpu.CompilerParams(
            collective_id=0, has_side_effects=True, vmem_limit_bytes=56 << 20
        ),
        cost_estimate=pl.CostEstimate(
            flops=6 * 512 * FEAT * UNITS, bytes_accessed=6 * FEAT * UNITS, transcendentals=64 * UNITS
        ),
    )(draft_lengths, states, gate_weight, up_weight, down_weight)
    return own + others


def solution(mesh):
    placed = (P("ffn", "hid"), P(), P("hid", "ffn"), P("hid", "ffn"), P("ffn", "hid"))
    return jax.shard_map(
        local, mesh=mesh, in_specs=placed, out_specs=P("ffn", "hid"), check_vma=False
    )
```
